512 devices in a mesh: vocab: 128 (over z, y, core), dp: 4 (over x).
Axes of the slice: x: 4, y: 8, z: 8, core: 2. Of those that a mesh axis runs over, the one named last changes fastest.
Arguments:
- teacher_hidden: bfloat16 [512, 4096], P(None, ('dp', 'vocab')), may hold values from -2200 to 2200
- student_hidden: bfloat16 [512, 4096], P(None, ('dp', 'vocab')), may hold values from -360 to 360
- teacher_head: bfloat16 [4096, 81920], P('dp', 'vocab'), may hold values from -0.09375 to 0.09375
- student_head: bfloat16 [4096, 81920], P('dp', 'vocab'), may hold values from -0.09375 to 0.09375
- token_ids: int32 [512], P('dp'), may hold values from 0 to 81919
- row_mask: int32 [512], P('dp'), may hold values from 0 to 1
Outputs:
- token_logprob: float32 [512], P('dp')
- loss: float32 [], replicated
- hidden_grad: bfloat16 [512, 4096], P(None, ('dp', 'vocab'))
- head_grad: bfloat16 [4096, 81920], P('dp', 'vocab')
The draws below stay inside these ranges and needn't reach their ends.
All inputs are finite; a program needn't handle non-finite values.
Results may differ from the reference program's by a relative error of at most 0.012.
Values may be sent and summed in bfloat16 or wider, within the bound.
A program may use at most 64 MiB of HBM per device.

```python
import jax
import jax.numpy as jnp

D = 4096
VOCAB = 81920
ROWS = 512


def scaled_rows(key, lowest, highest, rising):
    first, second = jax.random.split(key)
    base = jnp.clip(jax.random.normal(first, (ROWS, D), jnp.float32), -6.0, 6.0)
    scales = jnp.exp(jax.random.uniform(second, (ROWS, 1), jnp.float32, jnp.log(lowest), jnp.log(highest)))
    position = jnp.arange(ROWS, dtype=jnp.float32)[:, None] / ROWS
    return (base * scales * (1.0 + rising * position)).astype(jnp.bfloat16)


def draw_teacher_hidden(key, part):
    key = jax.random.fold_in(key, 11)
    return scaled_rows(key, 0.5, 4.0, 3.0)


def draw_student_hidden(key, part):
    key = jax.random.fold_in(key, 23)
    return scaled_rows(key, 0.5, 4.0, 0.0)


def draw_row_mask(key, part):
    key = jax.random.fold_in(key, 37)
    ticket = jax.random.randint(key, (ROWS,), 0, 4 * ROWS, jnp.int32)
    limit = ROWS + 3 * jnp.arange(ROWS, dtype=jnp.int32)
    return jnp.where(ticket < limit, 1, 0).astype(jnp.int32)


def set_ends(array, key, low, largest):
    shape = array.shape
    place = [jax.random.randint(jax.random.fold_in(key, axis), (), 0, shape[axis]) for axis in range(len(shape))]
    array = array.at[tuple(place)].set(low)
    longest = shape.index(max(shape))
    place[longest] = (place[longest] + 1) % shape[longest]
    return array.at[tuple(place)].set(largest)


def block_levels(key, shape, shards, least, largest):
    gain = 1.0
    for axis_at, blocks in shards:
        steps = jax.random.uniform(jax.random.fold_in(jax.random.fold_in(key, 6), axis_at), (blocks,), jnp.float32, least / len(shards), largest / len(shards))
        gain = gain * jnp.repeat(jnp.exp(steps), shape[axis_at] // blocks).reshape((-1,) + (1,) * (len(shape) - 1 - axis_at))
    return gain


def noise(stream_key, dims, width, most, cuts=(), kind=jnp.bfloat16):
    loudness = block_levels(stream_key, dims, cuts, -0.22, 0.18) if cuts else 1.0
    result = jax.random.normal(stream_key, dims, jnp.float32) * width * loudness
    return jnp.minimum(jnp.maximum(result, -most), most).astype(kind)


def setup_inputs(seed: int = 0) -> dict:
    arg_keys = jax.random.split(jax.random.key(seed), 7)
    return {
        "teacher_hidden": draw_teacher_hidden(jax.random.fold_in(arg_keys[6], 71), 0),
        "student_hidden": draw_student_hidden(jax.random.fold_in(arg_keys[6], 71), 0),
        "teacher_head": noise(arg_keys[2], (D, VOCAB), D ** -0.5, 0.09375, ((0, 4), (1, 128))),
        "student_head": noise(arg_keys[3], (D, VOCAB), D ** -0.5, 0.09375, ((0, 4), (1, 128))),
        "token_ids": set_ends(jax.random.randint(arg_keys[4], (ROWS,), 0, VOCAB), jax.random.fold_in(arg_keys[4], 1), 0, VOCAB - 1).astype(jnp.int32),
        "row_mask": draw_row_mask(jax.random.fold_in(arg_keys[6], 71), 0),
    }


def reference(teacher_hidden, student_hidden, teacher_head, student_head, token_ids, row_mask):
    teacher_logits = jnp.dot(teacher_hidden, teacher_head, preferred_element_type=jnp.float32)
    student_logits = jnp.dot(student_hidden, student_head, preferred_element_type=jnp.float32)
    teacher_lse = jax.nn.logsumexp(teacher_logits, axis=1, keepdims=True)
    student_lse = jax.nn.logsumexp(student_logits, axis=1, keepdims=True)
    student_logp = student_logits - student_lse
    teacher_logp = teacher_logits - teacher_lse
    probs = jnp.exp(student_logp)
    gap = student_logp - teacher_logp
    row_kl = jnp.sum(probs * gap, axis=1)
    token_logprob = jnp.take_along_axis(student_logp, token_ids[:, None].astype(jnp.int32), axis=1)[:, 0]
    weights = row_mask.astype(jnp.float32)
    loss = jnp.sum(weights * row_kl) / ROWS
    logit_grad = (weights[:, None] * probs * (gap - row_kl[:, None])).astype(jnp.bfloat16)
    hidden_grad = jnp.dot(logit_grad, student_head.T, preferred_element_type=jnp.float32).astype(jnp.bfloat16)
    head_grad = jnp.dot(student_hidden.T, logit_grad, preferred_element_type=jnp.float32).astype(jnp.bfloat16)
    return token_logprob, loss, hidden_grad, head_grad
```

```python
import functools

import jax
import jax.numpy as jnp
from jax import lax
from jax.experimental import pallas as pl
from jax.experimental.pallas import tpu as pltpu
from jax.sharding import PartitionSpec as P

F32 = jnp.float32
BF16 = jnp.bfloat16
NX = 4
LANES = 128


def combine(tiles):
    m_t = jnp.max(tiles[:, 0:1], axis=0)
    m_s = jnp.max(tiles[:, 2:3], axis=0)
    scale_t = jnp.exp(tiles[:, 0:1] - m_t[None])
    scale_s = jnp.exp(tiles[:, 2:3] - m_s[None])
    l_t = jnp.sum(tiles[:, 1:2] * scale_t, axis=0)
    l_s = jnp.sum(tiles[:, 3:4] * scale_s, axis=0)
    k_s = jnp.sum(tiles[:, 4:5] * scale_s, axis=0)
    label = jnp.sum(tiles[:, 5:6], axis=0)
    return m_t, l_t, m_s, l_s, k_s, label


def pack(parts):
    return jnp.concatenate(list(parts) + [jnp.zeros((2, LANES), F32)], axis=0)


def kernel(
    n, rows,
    th_ref, sh_ref, wt_hbm, ws_hbm, ids_ref, mask_ref,
    tok_ref, loss_ref, hid_ref, head_ref,
    own, gat, wt, ws, wtt, wst, xt, xs, part, hop, inc, sta, stb, gb, lossb,
    ht, sibr, sb, rb, sc, rc,
    lsem, s1, r1, s2, r2, s3, r3, sx, rx, ssa, rsa, ssb, rsb, sg, rg, sl, rl,
    s4, r4, s5, r5, s6, r6,
):
    width = wt.shape[1]
    v = lax.axis_index("vocab")
    x = lax.axis_index("dp")
    c = lax.rem(v, 2)
    y = lax.rem(v // 2, n)
    z = v // (2 * n)
    sibling = 1 - c

    def dev(zz, yy, cc, xx=None):
        return ((zz * n + yy) * 2 + cc, x if xx is None else xx)

    def remote(src, dst, send, recv, device):
        return pltpu.make_async_remote_copy(
            src_ref=src, dst_ref=dst, send_sem=send, recv_sem=recv,
            device_id=device, device_id_type=pl.DeviceIdType.MESH,
        )

    def each(count, body, start=1):
        lax.fori_loop(start, count, lambda i, carry: (body(i), carry)[1], 0)

    def step(pos, d):
        return lax.rem(pos + d, n)

    load_t = pltpu.make_async_copy(wt_hbm, wt, lsem.at[0])
    load_s = pltpu.make_async_copy(ws_hbm, ws, lsem.at[1])
    load_t.start()
    load_s.start()

    pair = y * 2 + c

    def group_dev(d):
        other = lax.rem(pair + d, 2 * n)
        return dev(z, other // 2, lax.rem(other, 2))

    barrier = pltpu.get_barrier_semaphore()

    def greet(device):
        pl.semaphore_signal(barrier, inc=1, device_id=device, device_id_type=pl.DeviceIdType.MESH)

    each(2 * n, lambda d: greet(group_dev(d)))
    each(n, lambda d: greet(dev(step(z, d), y, c)))
    each(NX, lambda d: greet(dev(z, y, c, lax.rem(x + d, NX))))

    chunk = [lax.rem(x + d, NX) for d in (2, 1, 3, 0)]
    right, left = chunk[1], chunk[2]
    for rel in range(NX):
        lanes = pl.ds(pl.multiple_of(chunk[rel] * LANES, LANES), LANES)
        block = jnp.concatenate([th_ref[:, lanes].astype(F32), sh_ref[:, lanes].astype(F32)], axis=0)
        own[rel] = block.astype(BF16)
    axes = [(z, y) if rel % 2 == 0 else (y, z) for rel in range(NX)]

    def along_p(rel, d):
        return dev(step(z, d), y, c) if rel % 2 == 0 else dev(z, step(y, d), c)

    def along_q(rel, d):
        return dev(z, step(y, d), c) if rel % 2 == 0 else dev(step(z, d), y, c)

    def first(rel, d):
        p, q = axes[rel]
        return remote(own.at[rel], gat.at[rel, c, p, q], s1.at[rel, d], r1.at[rel, d], along_q(rel, d))

    def second(rel, d):
        p, _ = axes[rel]
        return remote(gat.at[rel, c, p], gat.at[rel, c, p], s2.at[rel, d], r2.at[rel, d], along_p(rel, d))

    def swap(rel, d):
        p = lax.rem(axes[rel][0] + n - d, n)
        return remote(gat.at[rel, c, p], gat.at[rel, c, p], s3.at[rel, d], r3.at[rel, d], dev(z, y, sibling))

    pl.semaphore_wait(barrier, (2 * n - 1) + (n - 1) + (NX - 1))

    for rel in range(NX):
        each(n, lambda d: first(rel, d).start())
    for rel in range(NX):
        p, q = axes[rel]
        gat[rel, c, p, q] = own[rel]
    for rel in range(NX):
        each(n, lambda d: first(rel, d).wait_recv())
        each(n, lambda d: second(rel, d).start())
        swap(rel, 0).start()

    load_t.wait()
    load_s.wait()
    ones = (
        lax.broadcasted_iota(jnp.int32, (LANES, LANES), 0) == lax.broadcasted_iota(jnp.int32, (LANES, LANES), 1)
    ).astype(BF16)

    def turn(i):
        at = pl.ds(pl.multiple_of(i * LANES, LANES), LANES)
        for src, dst in ((wt, wtt), (ws, wst)):
            dst[at, :] = lax.dot_general(
                ones, src[:, at], (((1,), (1,)), ((), ())), preferred_element_type=F32
            ).astype(BF16)

    each(width // LANES, turn, 0)

    def logits(rel):
        def arrive(d):
            second(rel, d).wait_recv()
            swap(rel, d).start()

        each(n, arrive)
        each(n, lambda d: swap(rel, d).wait_recv(), 0)

        def place(i):
            a0, a1 = (gat[rel, k, i] if rel % 2 == 0 else gat[rel, k, :, i] for k in range(2))
            a0, a1 = a0.astype(F32), a1.astype(F32)
            at = pl.ds(pl.multiple_of(i * (n * 16), n * 16), n * 16)
            teacher = jnp.stack([a0[:, 0:8], a1[:, 0:8]], axis=1).reshape(n * 16, LANES)
            student = jnp.stack([a0[:, 8:16], a1[:, 8:16]], axis=1).reshape(n * 16, LANES)
            xt[at, :] = teacher.astype(BF16)
            xs[at, rel * LANES : (rel + 1) * LANES] = student.astype(BF16)

        each(n, place, 0)
        part[rel, 0] = jnp.dot(wtt[...], xt[...], preferred_element_type=F32)
        part[rel, 1] = jnp.dot(
            wst[...], xs[:, rel * LANES : (rel + 1) * LANES], preferred_element_type=F32
        )

    def ring(i, src, dst, to):
        return remote(src, dst, sx.at[i], rx.at[i], dev(z, y, c, to))

    x_copies = [
        ring(0, part.at[0, 0], hop.at[0], right),
        ring(1, part.at[0, 1], hop.at[1], left),
        ring(2, part.at[1, 1], inc.at[0, 1], right),
        ring(3, part.at[2, 0], inc.at[1, 0], left),
        ring(4, part.at[1, 0], inc.at[0, 0], right),
        ring(5, part.at[2, 1], inc.at[1, 1], left),
    ]
    logits(0)
    x_copies[0].start()
    x_copies[1].start()
    logits(1)
    x_copies[2].start()
    logits(2)
    x_copies[3].start()
    x_copies[0].wait_recv()
    part[1, 0] = part[1, 0] + hop[0]
    x_copies[4].start()
    x_copies[1].wait_recv()
    part[2, 1] = part[2, 1] + hop[1]
    x_copies[5].start()
    logits(3)
    for i in (2, 3, 4, 5):
        x_copies[i].wait_recv()
    t = part[3, 0] + inc[0, 0] + inc[1, 0]
    s = part[3, 1] + inc[0, 1] + inc[1, 1]

    m_t = jnp.max(t, axis=0, keepdims=True)
    m_s = jnp.max(s, axis=0, keepdims=True)
    l_t = jnp.sum(jnp.exp(t - m_t), axis=0, keepdims=True)
    e_s = jnp.exp(s - m_s)
    l_s = jnp.sum(e_s, axis=0, keepdims=True)
    k_s = jnp.sum(e_s * (s - t), axis=0, keepdims=True)
    is_label = lax.broadcasted_iota(jnp.int32, (width, LANES), 0) == ids_ref[...] - v * width
    label = jnp.sum(jnp.where(is_label, s, 0.0), axis=0, keepdims=True)
    sta[pair] = pack((m_t, l_t, m_s, l_s, k_s, label))

    def stat_a(d):
        return remote(sta.at[pair], sta.at[pair], ssa.at[d], rsa.at[d], group_dev(d))

    def stat_b(d):
        return remote(stb.at[z], stb.at[z], ssb.at[d], rsb.at[d], dev(step(z, d), y, c))

    each(2 * n, lambda d: stat_a(d).start())
    each(2 * n, lambda d: stat_a(d).wait_recv())
    stb[z] = pack(combine(sta[...]))
    each(n, lambda d: stat_b(d).start())
    each(n, lambda d: stat_b(d).wait_recv())
    m_t, l_t, m_s, l_s, k_s, label = combine(stb[...])
    lse_t = m_t + jnp.log(l_t)
    lse_s = m_s + jnp.log(l_s)
    row_kl = k_s / l_s - lse_s + lse_t
    weights = mask_ref[...].astype(F32)
    logp = s - lse_s
    gap = logp - (t - lse_t)
    gb[:, 3 * LANES :] = (weights * jnp.exp(logp) * (gap - row_kl)).astype(BF16)
    tok_ref[...] = label - lse_s

    def slot(i):
        return slice(i * LANES, (i + 1) * LANES)

    half = width // 2
    g_copies = [
        remote(gb.at[:, slot(3)], gb.at[:, slot(2)], sg.at[0], rg.at[0], dev(z, y, c, right)),
        remote(gb.at[:, slot(3)], gb.at[:, slot(1)], sg.at[1], rg.at[1], dev(z, y, c, left)),
        remote(gb.at[0:half, slot(2)], gb.at[0:half, slot(0)], sg.at[2], rg.at[2], dev(z, y, c, right)),
        remote(gb.at[half:, slot(1)], gb.at[half:, slot(0)], sg.at[3], rg.at[3], dev(z, y, c, left)),
    ]
    g_copies[0].start()
    g_copies[1].start()

    def loss_copy(d):
        return remote(lossb.at[x], lossb.at[x], sl.at[d], rl.at[d], dev(z, y, c, lax.rem(x + d, NX)))

    lossb[x] = jnp.broadcast_to(weights * row_kl, (8, LANES))
    each(NX, lambda d: loss_copy(d).start())

    def core_copy(i):
        return remote(ht.at[i, :, sibling], sibr.at[i], s4.at[i], r4.at[i], dev(z, y, sibling))

    def terms(i):
        ht[i] = jnp.dot(ws[...], gb[:, slot(i)], preferred_element_type=F32).reshape(n * n, 2, 8, LANES)
        core_copy(i).start()

    def outer(i, d):
        p, _ = axes[i]
        return remote(sb.at[i, step(p, d)], rb.at[i, p], s5.at[i, d], r5.at[i, d], along_p(i, d))

    def inner(i, d):
        _, q = axes[i]
        return remote(sc.at[i, step(q, d)], rc.at[i, q], s6.at[i, d], r6.at[i, d], along_q(i, d))

    def send_outer(i):
        p, _ = axes[i]
        core_copy(i).wait_recv()
        total = (ht[i, :, c] + sibr[i]).reshape(n, n, 8, LANES)
        for k in range(n):
            piece = total[k] if i % 2 == 0 else total[:, k]
            sb[i, k] = piece.reshape(n * 8, LANES).astype(BF16)
        each(n, lambda d: outer(i, d).start())
        rb[i, p] = sb[i, p]

    def send_inner(i):
        _, q = axes[i]
        each(n, lambda d: outer(i, d).wait_recv())
        sc[i] = jnp.sum(rb[i].astype(F32), axis=0).reshape(n, 8, LANES)
        each(n, lambda d: inner(i, d).start())
        rc[i, q] = sc[i, q]

    def finish(i):
        each(n, lambda d: inner(i, d).wait_recv())
        lanes = pl.ds(pl.multiple_of(chunk[i] * LANES, LANES), LANES)
        hid_ref[:, lanes] = jnp.sum(rc[i], axis=0).astype(BF16)

    terms(3)
    g_copies[0].wait_recv()
    g_copies[2].start()
    g_copies[1].wait_recv()
    g_copies[3].start()
    send_outer(3)
    terms(2)
    terms(1)
    send_outer(2)
    send_outer(1)
    g_copies[2].wait_recv()
    g_copies[3].wait_recv()
    terms(0)
    send_outer(0)
    each(NX, lambda d: loss_copy(d).wait_recv())
    loss = jnp.sum(lossb[:, 0:1].reshape(NX, LANES)) / rows
    loss_ref[...] = jnp.full((8, LANES), loss, F32)
    head_ref[...] = lax.dot_general(
        xs[...], gb[...], (((1,), (1,)), ((), ())), preferred_element_type=F32
    ).astype(BF16)
    for i in (3, 2, 1, 0):
        send_inner(i)
    for i in (3, 2, 1, 0):
        finish(i)

    for rel in range(NX):
        each(n, lambda d: first(rel, d).wait_send())
        each(n, lambda d: second(rel, d).wait_send())
        each(n, lambda d: swap(rel, d).wait_send(), 0)
        core_copy(rel).wait_send()
        each(n, lambda d: outer(rel, d).wait_send())
        each(n, lambda d: inner(rel, d).wait_send())
    for copy in x_copies + g_copies:
        copy.wait_send()
    each(2 * n, lambda d: stat_a(d).wait_send())
    each(n, lambda d: stat_b(d).wait_send())
    each(NX, lambda d: loss_copy(d).wait_send())


def shards(n, teacher_hidden, student_hidden, teacher_head, student_head, token_ids, row_mask):
    rows = teacher_hidden.shape[0]
    depth, width = teacher_head.shape
    vmem = pl.BlockSpec(memory_space=pltpu.VMEM)
    hbm = pl.BlockSpec(memory_space=pl.ANY)
    dma = pltpu.SemaphoreType.DMA
    scratch = [
        pltpu.VMEM((NX, 16, LANES), BF16),
        pltpu.VMEM((NX, 2, n, n, 16, LANES), BF16),
        pltpu.VMEM((depth, width), BF16),
        pltpu.VMEM((depth, width), BF16),
        pltpu.VMEM((width, depth), BF16),
        pltpu.VMEM((width, depth), BF16),
        pltpu.VMEM((depth, LANES), BF16),
        pltpu.VMEM((depth, rows), BF16),
        pltpu.VMEM((NX, 2, width, LANES), F32),
        pltpu.VMEM((2, width, LANES), F32),
        pltpu.VMEM((2, 2, width, LANES), F32),
        pltpu.VMEM((2 * n, 8, LANES), F32),
        pltpu.VMEM((n, 8, LANES), F32),
        pltpu.VMEM((width, rows), BF16),
        pltpu.VMEM((NX, 8, LANES), F32),
        pltpu.VMEM((NX, n * n, 2, 8, LANES), F32),
        pltpu.VMEM((NX, n * n, 8, LANES), F32),
        pltpu.VMEM((NX, n, n * 8, LANES), BF16),
        pltpu.VMEM((NX, n, n * 8, LANES), BF16),
        pltpu.VMEM((NX, n, 8, LANES), F32),
        pltpu.VMEM((NX, n, 8, LANES), F32),
        dma((2,)),
        dma((NX, n)), dma((NX, n)),
        dma((NX, n)), dma((NX, n)),
        dma((NX, n)), dma((NX, n)),
        dma((6,)), dma((6,)),
        dma((2 * n,)), dma((2 * n,)),
        dma((n,)), dma((n,)),
        dma((4,)), dma((4,)),
        dma((NX,)), dma((NX,)),
        dma((NX,)), dma((NX,)),
        dma((NX, n)), dma((NX, n)),
        dma((NX, n)), dma((NX, n)),
    ]
    tok, loss, hidden, head = pl.pallas_call(
        functools.partial(kernel, n, rows),
        out_shape=(
            jax.ShapeDtypeStruct((1, LANES), F32),
            jax.ShapeDtypeStruct((8, LANES), F32),
            jax.ShapeDtypeStruct((8, rows), BF16),
            jax.ShapeDtypeStruct((depth, width), BF16),
        ),
        in_specs=[vmem, vmem, hbm, hbm, vmem, vmem],
        out_specs=(vmem,) * 4,
        scratch_shapes=scratch,
        compiler_params=pltpu.CompilerParams(
            collective_id=0, has_side_effects=True, vmem_limit_bytes=48 * 1024 * 1024
        ),
        cost_estimate=pl.CostEstimate(flops=6 * 10**9, bytes_accessed=5 * 10**6, transcendentals=3 * 10**5),
    )(
        teacher_hidden.T, student_hidden.T, teacher_head, student_head,
        token_ids.reshape(1, LANES), row_mask.reshape(1, LANES),
    )
    return (tok.reshape(LANES), loss[0, 0], hidden.T, head)


def solution(mesh):
    side = int(round((mesh.shape["vocab"] // 2) ** 0.5))
    placed = (
        P(None, ("dp", "vocab")),
        P(None, ("dp", "vocab")),
        P("dp", "vocab"),
        P("dp", "vocab"),
        P("dp"),
        P("dp"),
    )
    return jax.shard_map(
        functools.partial(shards, side),
        mesh=mesh,
        in_specs=placed,
        out_specs=(P("dp"), P(), P(None, ("dp", "vocab")), P("dp", "vocab")),
        check_vma=False,
    )
```

```python
import functools

import jax
import jax.numpy as jnp
from jax import lax
from jax.experimental import pallas as pl
from jax.experimental.pallas import tpu as pltpu
from jax.sharding import PartitionSpec as P

F32 = jnp.float32
BF16 = jnp.bfloat16
NX = 4
LANES = 128


def code(values):
    top = jnp.maximum(jnp.max(jnp.abs(values), axis=0, keepdims=True), 1e-30)
    scaled = values * (32767.0 / top)
    whole = (scaled + jnp.where(scaled >= 0.0, 0.5, -0.5)).astype(jnp.int32)
    return whole.astype(jnp.int16), jnp.broadcast_to(top / 32767.0, (8, LANES))


def decode(coded, scale):
    return coded.astype(jnp.int32).astype(F32) * scale[0:1]


def combine(stats):
    tops, sums, extras = (stats[:, :, i * LANES : (i + 1) * LANES] for i in range(3))
    top = jnp.max(tops, axis=0)
    scale = jnp.exp(tops - top[None])
    return top, jnp.sum(sums * scale, axis=0), jnp.sum(extras * scale, axis=0), jnp.sum(extras, axis=0)


def kernel(
    n, rows,
    th_hbm, sh_hbm, wt_hbm, ws_hbm, ids_hbm, mask_hbm,
    tok_ref, loss_ref, hid_ref, head_ref,
    th_ref, sh_ref, ids_ref, mask_ref,
    own, gat, wt, ws, wtt, wst, xt, xs, part, diff, unit, hop_s, hop_d, hop_u, inc_s, inc_d, inc_u, sta, stb, tta, ttb, gb, grad, coef, lossb,
    ht, sibr, sb, rb, sc, rc,
    lsem, sent, r1, r2, r3, r4, r5, r6, rx, rg, rs,
):
    width = wt.shape[1]
    v = lax.axis_index("vocab")
    x = lax.axis_index("dp")
    c = lax.rem(v, 2)
    y = lax.rem(v // 2, n)
    z = v // (2 * n)
    sibling = 1 - c

    def dev(zz, yy, cc, xx=None):
        return ((zz * n + yy) * 2 + cc, x if xx is None else xx)

    def remote(src, dst, send, recv, device):
        return pltpu.make_async_remote_copy(
            src_ref=src, dst_ref=dst, send_sem=send, recv_sem=recv,
            device_id=device, device_id_type=pl.DeviceIdType.MESH,
        )

    def each(count, body, start=1):
        lax.fori_loop(start, count, lambda i, carry: (body(i), carry)[1], 0)

    def step(pos, d):
        return lax.rem(pos + d, n)

    first_s, second_s, swap_s, core_s, outer_s, inner_s, stat_a_s, stat_b_s, loss_s, g_s, logit_s, diff_s, teacher_a_s, teacher_b_s, coef_s, unit_s = (
        sent.at[i] for i in range(16)
    )

    def await_bytes(view, sem):
        pltpu.make_async_copy(view, view, sem).wait()

    local = [
        pltpu.make_async_copy(src, dst, lsem.at[i])
        for i, (src, dst) in enumerate((
            (th_hbm, th_ref), (sh_hbm, sh_ref), (wt_hbm, wt), (ws_hbm, ws), (ids_hbm, ids_ref), (mask_hbm, mask_ref),
        ))
    ]
    for i in range(6):
        local[i].start()

    pair = y * 2 + c

    def group_dev(d):
        other = lax.rem(pair + d, 2 * n)
        return dev(z, other // 2, lax.rem(other, 2))

    barrier = pltpu.get_barrier_semaphore()

    def greet(device):
        pl.semaphore_signal(barrier, inc=1, device_id=device, device_id_type=pl.DeviceIdType.MESH)

    each(2 * n, lambda d: greet(group_dev(d)))
    each(n, lambda d: greet(dev(step(z, d), y, c)))
    each(NX, lambda d: greet(dev(z, y, c, lax.rem(x + d, NX))))

    chunk = [lax.rem(x + d, NX) for d in (2, 1, 3, 0)]
    right, left = chunk[1], chunk[2]
    local[0].wait()
    local[1].wait()
    for rel in range(NX):
        lanes = pl.ds(pl.multiple_of(chunk[rel] * LANES, LANES), LANES)
        block = jnp.concatenate([th_ref[:, lanes].astype(F32), sh_ref[:, lanes].astype(F32)], axis=0)
        own[rel] = block.astype(BF16)
    flip = c
    p, q = (1 - flip) * z + flip * y, (1 - flip) * y + flip * z

    def along_p(d):
        return dev(step(z, d * (1 - flip)), step(y, d * flip), c)

    def along_q(d):
        return dev(step(z, d * flip), step(y, d * (1 - flip)), c)

    def first(cut, sem, d):
        return remote(own.at[cut], gat.at[cut, c, p, q], first_s, sem, along_q(d))

    def second(rel, sem, d):
        return remote(gat.at[rel, c, p], gat.at[rel, c, p], second_s, r2.at[rel, sem], along_p(d))

    def swap(rel, d):
        at = lax.rem(p + n - d, n)
        return remote(gat.at[rel, c, at], gat.at[rel, c, at], swap_s, r3.at[rel], dev(z, y, sibling))

    pl.semaphore_wait(barrier, (2 * n - 1) + (n - 1) + (NX - 1))

    near = [d for d in range(1, n) if min(d, n - d) <= n // 4]
    far = [d for d in range(1, n) if d not in near]
    lead, rest = slice(0, 1), slice(1, NX)
    each(n, lambda d: first(lead, r1.at[0], d).start())
    each(n, lambda d: first(rest, r1.at[1], d).start())
    for rel in range(NX):
        gat[rel, c, p, q] = own[rel]

    def spread(rel):
        for d in far:
            second(rel, 1, d).start()
        for d in near:
            second(rel, 0, d).start()
        swap(rel, 0).start()

    await_bytes(gat.at[lead, 0, 0, 0 : n - 1], r1.at[0])
    spread(0)
    await_bytes(gat.at[rest, 0, 0, 0 : n - 1], r1.at[1])
    for rel in range(1, NX):
        spread(rel)

    for i in range(2, 6):
        local[i].wait()
    ones = (
        lax.broadcasted_iota(jnp.int32, (LANES, LANES), 0) == lax.broadcasted_iota(jnp.int32, (LANES, LANES), 1)
    ).astype(BF16)

    def turn(i):
        at = pl.ds(pl.multiple_of(i * LANES, LANES), LANES)
        for src, dst in ((wt, wtt), (ws, wst)):
            dst[at, :] = lax.dot_general(
                ones, src[:, at], (((1,), (1,)), ((), ())), preferred_element_type=F32
            ).astype(BF16)

    each(width // LANES, turn, 0)

    half = width // 2
    upper, lower = slice(0, half), slice(half, width)

    def logits(rel, after_student=lambda: None):
        for sem, group in ((0, near), (1, far)):
            if group:
                await_bytes(gat.at[rel, 0, 0 : len(group)], r2.at[rel, sem])
            for d in group:
                swap(rel, d).start()
        await_bytes(gat.at[rel, 0], r3.at[rel])

        def place(i):
            a0, a1 = gat[rel, 0, i].astype(F32), gat[rel, 1, :, i].astype(F32)
            at = pl.ds(pl.multiple_of(i * (n * 16), n * 16), n * 16)
            teacher = jnp.stack([a0[:, 0:8], a1[:, 0:8]], axis=1).reshape(n * 16, LANES)
            student = jnp.stack([a0[:, 8:16], a1[:, 8:16]], axis=1).reshape(n * 16, LANES)
            xt[at, :] = teacher.astype(BF16)
            xs[at, rel * LANES : (rel + 1) * LANES] = student.astype(BF16)

        each(n, place, 0)
        student = jnp.dot(wst[...], xs[:, rel * LANES : (rel + 1) * LANES], preferred_element_type=F32)
        part[rel, 1] = student
        after_student()
        part[rel, 0] = student - jnp.dot(wtt[...], xt[...], preferred_element_type=F32)
        if rel == 0:
            diff[0], unit[0] = code(part[0, 0])
        elif rel < NX - 1:
            early_rows = lower if rel == 1 else upper
            diff[rel, early_rows], unit[rel] = code(part[rel, 0, early_rows])

    def ring(src, dst, send, recv, to):
        return remote(src, dst, send, recv, dev(z, y, c, to))

    def hop_pair(cut, way, to):
        return [
            ring(part.at[0, 1, cut], hop_s.at[way], logit_s, rx.at[way], to),
            ring(unit.at[0], hop_u.at[way], unit_s, rx.at[6 + way], to),
            ring(diff.at[0, cut], hop_d.at[way], diff_s, rx.at[2 + way], to),
        ]

    def last_pair(rel, cut, way, to, unit_at):
        return [
            ring(part.at[rel, 1, cut], inc_s.at[way, cut], logit_s, rx.at[4], to),
            ring(unit.at[unit_at], inc_u.at[way, 0 if cut == upper else 1], unit_s, rx.at[8], to),
            ring(diff.at[rel, cut], inc_d.at[way, cut], diff_s, rx.at[5], to),
        ]

    hops = [hop_pair(upper, 0, right), hop_pair(lower, 1, left)]
    early = [last_pair(1, lower, 0, right, 1), last_pair(2, upper, 1, left, 2)]
    late = [last_pair(1, upper, 0, right, 3), last_pair(2, lower, 1, left, 4)]

    def start(*copies):
        for copy in copies:
            copy.start()

    def add_hop(way, rel, cut):
        hops[way][0].wait_recv()
        part[rel, 1, cut] = part[rel, 1, cut] + hop_s[way]
        late[way][0].start()
        hops[way][1].wait_recv()
        hops[way][2].wait_recv()
        diff[rel, cut], unit[3 + way] = code(part[rel, 0, cut] + decode(hop_d[way], hop_u[way]))
        start(*late[way][1:])

    logits(0, lambda: start(hops[0][0], hops[1][0]))
    start(*hops[0][1:], *hops[1][1:])
    logits(1, lambda: start(early[0][0]))
    start(*early[0][1:])
    logits(2, lambda: start(early[1][0]))
    start(*early[1][1:])
    add_hop(0, 1, upper)
    add_hop(1, 2, lower)
    logits(3)
    await_bytes(inc_s, rx.at[4])
    await_bytes(inc_d, rx.at[5])
    await_bytes(inc_u, rx.at[8])
    s = part[3, 1] + inc_s[0] + inc_s[1]
    gap = jnp.concatenate(
        [
            part[3, 0, cut] + decode(inc_d[0, cut], inc_u[0, k]) + decode(inc_d[1, cut], inc_u[1, k])
            for k, cut in enumerate((upper, lower))
        ],
        axis=0,
    )

    def stat_a(buf, send, sem, d):
        return remote(buf.at[pair], buf.at[pair], send, sem, group_dev(d))

    def stat_b(buf, send, sem, d):
        return remote(buf.at[z], buf.at[z], send, sem, dev(step(z, d), y, c))

    def send_a(buf, send, sem, parts):
        buf[pair] = jnp.concatenate(parts, axis=1)
        each(2 * n, lambda d: stat_a(buf, send, sem, d).start())

    def send_b(buf, send, sem, parts):
        buf[z] = jnp.concatenate(parts, axis=1)
        each(n, lambda d: stat_b(buf, send, sem, d).start())

    def slot(i):
        return slice(i * LANES, (i + 1) * LANES)

    quarter = half // 2
    cuts = [slice(k * quarter, (k + 1) * quarter) for k in range(4)]

    def g_copy(i, part_rows, source, target, to):
        return ring(gb.at[:, part_rows, slot(source)], gb.at[:, part_rows, slot(target)], g_s, rg.at[i], to)

    g_lead = [
        g_copy(0, cuts[0], 3, 2, right),
        g_copy(1, cuts[2], 3, 1, left),
        g_copy(2, cuts[1], 3, 2, right),
        g_copy(3, cuts[3], 3, 1, left),
    ]
    g_rest = [g_copy(4, lower, 3, 2, right), g_copy(5, upper, 3, 1, left)]
    g_relay = [
        g_copy(6, cuts[0], 2, 0, right),
        g_copy(6, cuts[2], 1, 0, left),
        g_copy(6, cuts[1], 2, 0, right),
        g_copy(6, cuts[3], 1, 0, left),
    ]
    m_s = jnp.max(s, axis=0, keepdims=True)
    e_s = jnp.exp(s - m_s)
    l_s = jnp.sum(e_s, axis=0, keepdims=True)
    k_s = jnp.sum(e_s * gap, axis=0, keepdims=True)
    send_a(sta, stat_a_s, rs.at[0], (m_s, l_s, k_s))
    own_top, own_mean = m_s, k_s / l_s
    gb[0, :, slot(3)] = e_s.astype(BF16)
    gb[1, :, slot(3)] = (e_s * (gap - own_mean)).astype(BF16)
    start(*g_lead, *g_rest)
    t = s - gap
    m_t = jnp.max(t, axis=0, keepdims=True)
    l_t = jnp.sum(jnp.exp(t - m_t), axis=0, keepdims=True)
    is_label = lax.broadcasted_iota(jnp.int32, (width, LANES), 0) == ids_ref[...] - v * width
    label = jnp.sum(jnp.where(is_label, s, 0.0), axis=0, keepdims=True)
    send_a(tta, teacher_a_s, rs.at[3], (m_t, l_t, label))
    await_bytes(sta.at[0 : 2 * n - 1], rs.at[0])
    send_b(stb, stat_b_s, rs.at[1], combine(sta[...])[:3])
    for k in range(4):
        g_lead[k].wait_recv()
        g_relay[k].start()
    await_bytes(tta.at[0 : 2 * n - 1], rs.at[3])
    m_t, l_t, _, label = combine(tta[...])
    send_b(ttb, teacher_b_s, rs.at[4], (m_t, l_t, label))
    await_bytes(stb.at[0 : n - 1], rs.at[1])
    m_s, l_s, k_s, _ = combine(stb[...])
    lse_s = m_s + jnp.log(l_s)
    mean_gap = k_s / l_s
    weights = mask_ref[...].astype(F32)
    factor = weights * jnp.exp(own_top - lse_s)
    coef[3] = jnp.concatenate([factor, factor * (mean_gap - own_mean), jnp.zeros((6, LANES), F32)], axis=0)
    coef_copies = [
        ring(coef.at[3], coef.at[0], coef_s, rs.at[5], chunk[0]),
        ring(coef.at[3], coef.at[2], coef_s, rs.at[7], right),
        ring(coef.at[3], coef.at[1], coef_s, rs.at[6], left),
    ]
    start(*coef_copies)

    def gradient(i):
        scale, shift = coef[i, 0:1], coef[i, 1:2]
        grad[:, slot(i)] = (
            scale * gb[1, :, slot(i)].astype(F32) - shift * gb[0, :, slot(i)].astype(F32)
        ).astype(BF16)

    def loss_copy(d):
        return remote(lossb.at[x], lossb.at[x], loss_s, rs.at[2], dev(z, y, c, lax.rem(x + d, NX)))

    def send_loss():
        await_bytes(ttb.at[0 : n - 1], rs.at[4])
        m_t, l_t, _, label = combine(ttb[...])
        tok_ref[...] = label - lse_s
        row_kl = mean_gap - lse_s + m_t + jnp.log(l_t)
        lossb[x] = jnp.broadcast_to(weights * row_kl, (8, LANES))
        each(NX, lambda d: loss_copy(d).start())

    def core_copy(i):
        return remote(ht.at[i, :, sibling], sibr.at[i], core_s, r4.at[i], dev(z, y, sibling))

    def terms(i):
        gradient(i)
        ht[i] = jnp.dot(ws[...], grad[:, slot(i)], preferred_element_type=F32).reshape(n * n, 2, 8, LANES)
        core_copy(i).start()

    def outer(i, d):
        return remote(sb.at[i, step(p, d)], rb.at[i, p], outer_s, r5.at[i], along_p(d))

    def inner(i, d):
        return remote(sc.at[i, step(q, d)], rc.at[i, q], inner_s, r6.at[i], along_q(d))

    def send_outer(i):
        core_copy(i).wait_recv()
        total = (ht[i, :, c] + sibr[i]).reshape(n, n, 8, LANES)
        for k in range(n):
            piece = jnp.where(c == 0, total[k], total[:, k])
            sb[i, k] = piece.reshape(n * 8, LANES).astype(BF16)
        each(n, lambda d: outer(i, d).start())
        rb[i, p] = sb[i, p]

    def send_inner(i):
        await_bytes(rb.at[i, 0 : n - 1], r5.at[i])
        sc[i] = jnp.sum(rb[i].astype(F32), axis=0).reshape(n, 8, LANES)
        each(n, lambda d: inner(i, d).start())
        rc[i, q] = sc[i, q]

    def finish(i):
        await_bytes(rc.at[i, 0 : n - 1], r6.at[i])
        lanes = pl.ds(pl.multiple_of(chunk[i] * LANES, LANES), LANES)
        hid_ref[:, lanes] = jnp.sum(rc[i], axis=0)

    terms(3)
    send_loss()
    send_outer(3)
    g_rest[0].wait_recv()
    coef_copies[1].wait_recv()
    terms(2)
    g_rest[1].wait_recv()
    coef_copies[2].wait_recv()
    terms(1)
    send_outer(2)
    send_outer(1)
    await_bytes(gb.at[:, :, slot(0)], rg.at[6])
    coef_copies[0].wait_recv()
    terms(0)
    send_outer(0)
    await_bytes(lossb.at[0 : NX - 1], rs.at[2])
    loss = jnp.sum(lossb[:, 0:1].reshape(NX, LANES)) / rows
    loss_ref[...] = jnp.full((1, LANES), loss, F32)
    head_ref[...] = lax.dot_general(
        xs[...], grad[...], (((1,), (1,)), ((), ())), preferred_element_type=F32
    ).astype(BF16)
    for i in (3, 2, 1, 0):
        send_inner(i)
    for i in (3, 2, 1, 0):
        finish(i)

    for view, sem in (
        (gat.at[:, 0, 0, 0 : n - 1], first_s),
        (gat.at[:, 0, 0 : n - 1], second_s),
        (gat.at[:, 0], swap_s),
        (sibr, core_s),
        (sb.at[:, 0 : n - 1], outer_s),
        (sc.at[:, 0 : n - 1], inner_s),
        (sta.at[0 : 2 * n - 1], stat_a_s),
        (tta.at[0 : 2 * n - 1], teacher_a_s),
        (stb.at[0 : n - 1], stat_b_s),
        (ttb.at[0 : n - 1], teacher_b_s),
        (lossb.at[0 : NX - 1], loss_s),
        (gb.at[:, :, 0 : 3 * LANES], g_s),
        (coef.at[0 : NX - 1], coef_s),
        (part.at[0 : NX - 1, 1], logit_s),
        (diff, diff_s),
        (unit, unit_s),
    ):
        await_bytes(view, sem)


def store(tok_ref, loss_ref, hid_ref, head_ref, tok_out, loss_out, hid_out, head_out, one, rounded, sems):
    copies = [
        pltpu.make_async_copy(src, dst, sems.at[i])
        for i, (src, dst) in enumerate(
            ((head_ref, head_out), (tok_ref, tok_out), (one, loss_out), (rounded, hid_out))
        )
    ]
    copies[0].start()
    copies[1].start()
    one[...] = loss_ref[:, 0:1]
    rounded[...] = hid_ref[...].astype(BF16)
    copies[2].start()
    copies[3].start()
    for copy in copies:
        copy.wait()


def shards(n, teacher_hidden, student_hidden, teacher_head, student_head, token_ids, row_mask):
    rows = teacher_hidden.shape[0]
    depth, width = teacher_head.shape
    hbm = pl.BlockSpec(memory_space=pl.ANY)
    dma = pltpu.SemaphoreType.DMA
    scratch = [
        pltpu.VMEM((8, rows), BF16),
        pltpu.VMEM((8, rows), BF16),
        pltpu.VMEM((1, LANES), jnp.int32),
        pltpu.VMEM((1, LANES), jnp.int32),
        pltpu.VMEM((NX, 16, LANES), BF16),
        pltpu.VMEM((NX, 2, n, n, 16, LANES), BF16),
        pltpu.VMEM((depth, width), BF16),
        pltpu.VMEM((depth, width), BF16),
        pltpu.VMEM((width, depth), BF16),
        pltpu.VMEM((width, depth), BF16),
        pltpu.VMEM((depth, LANES), BF16),
        pltpu.VMEM((depth, rows), BF16),
        pltpu.VMEM((NX, 2, width, LANES), F32),
        pltpu.VMEM((NX - 1, width, LANES), jnp.int16),
        pltpu.VMEM((6, 8, LANES), F32),
        pltpu.VMEM((2, width // 2, LANES), F32),
        pltpu.VMEM((2, width // 2, LANES), jnp.int16),
        pltpu.VMEM((2, 8, LANES), F32),
        pltpu.VMEM((2, width, LANES), F32),
        pltpu.VMEM((2, width, LANES), jnp.int16),
        pltpu.VMEM((2, 2, 8, LANES), F32),
        pltpu.VMEM((2 * n, 1, 3 * LANES), F32),
        pltpu.VMEM((n, 1, 3 * LANES), F32),
        pltpu.VMEM((2 * n, 1, 3 * LANES), F32),
        pltpu.VMEM((n, 1, 3 * LANES), F32),
        pltpu.VMEM((2, width, rows), BF16),
        pltpu.VMEM((width, rows), BF16),
        pltpu.VMEM((NX, 8, LANES), F32),
        pltpu.VMEM((NX, 8, LANES), F32),
        pltpu.VMEM((NX, n * n, 2, 8, LANES), F32),
        pltpu.VMEM((NX, n * n, 8, LANES), F32),
        pltpu.VMEM((NX, n, n * 8, LANES), BF16),
        pltpu.VMEM((NX, n, n * 8, LANES), BF16),
        pltpu.VMEM((NX, n, 8, LANES), F32),
        pltpu.VMEM((NX, n, 8, LANES), F32),
        dma((6,)), dma((16,)), dma((2,)), dma((NX, 2)), dma((NX,)), dma((NX,)), dma((NX,)), dma((NX,)),
        dma((9,)), dma((7,)), dma((8,)),
    ]
    tok, loss, hidden, head = pl.pallas_call(
        functools.partial(kernel, n, rows),
        out_shape=(
            pltpu.VMEM((1, LANES), F32),
            pltpu.VMEM((1, LANES), F32),
            pltpu.VMEM((8, rows), F32),
            pltpu.VMEM((depth, width), BF16),
        ),
        in_specs=[hbm] * 6,
        out_specs=(pl.BlockSpec(memory_space=pltpu.VMEM),) * 4,
        scratch_shapes=scratch,
        compiler_params=pltpu.CompilerParams(
            collective_id=0, has_side_effects=True, vmem_limit_bytes=60 * 1024 * 1024
        ),
        cost_estimate=pl.CostEstimate(flops=6 * 10**9, bytes_accessed=5 * 10**6, transcendentals=3 * 10**5),
    )(
        teacher_hidden.T, student_hidden.T, teacher_head, student_head,
        token_ids.reshape(1, LANES), row_mask.reshape(1, LANES),
    )
    vmem = pl.BlockSpec(memory_space=pltpu.VMEM)
    tok, loss, hidden, head = pl.pallas_call(
        store,
        out_shape=(
            jax.ShapeDtypeStruct((1, LANES), F32),
            jax.ShapeDtypeStruct((1, 1), F32),
            jax.ShapeDtypeStruct((8, rows), BF16),
            jax.ShapeDtypeStruct((depth, width), BF16),
        ),
        in_specs=[vmem] * 4,
        out_specs=(hbm,) * 4,
        scratch_shapes=[pltpu.VMEM((1, 1), F32), pltpu.VMEM((8, rows), BF16), dma((4,))],
        compiler_params=pltpu.CompilerParams(vmem_limit_bytes=4 * 1024 * 1024),
    )(tok, loss, hidden, head)
    return (tok.reshape(LANES), loss.reshape(()), hidden.T, head)


def solution(mesh):
    side = int(round((mesh.shape["vocab"] // 2) ** 0.5))
    placed = (
        P(None, ("dp", "vocab")),
        P(None, ("dp", "vocab")),
        P("dp", "vocab"),
        P("dp", "vocab"),
        P("dp"),
        P("dp"),
    )
    return jax.shard_map(
        functools.partial(shards, side),
        mesh=mesh,
        in_specs=placed,
        out_specs=(P("dp"), P(), P(None, ("dp", "vocab")), P("dp", "vocab")),
        check_vma=False,
    )
```

```python
import functools

import jax
import jax.numpy as jnp
from jax import lax
from jax.experimental import pallas as pl
from jax.experimental.pallas import tpu as pltpu
from jax.sharding import PartitionSpec as P

F32 = jnp.float32
BF16 = jnp.bfloat16
NX = 4
LANES = 128


def code(values):
    top = jnp.maximum(jnp.max(jnp.abs(values), axis=0, keepdims=True), 1e-30)
    scaled = values * (32767.0 / top)
    whole = (scaled + jnp.where(scaled >= 0.0, 0.5, -0.5)).astype(jnp.int32)
    return whole.astype(jnp.int16), jnp.broadcast_to(top / 32767.0, (8, LANES))


def decode(coded, scale):
    return coded.astype(jnp.int32).astype(F32) * scale[0:1]


def combine(stats):
    tops, sums, extras = (stats[:, :, i * LANES : (i + 1) * LANES] for i in range(3))
    top = jnp.max(tops, axis=0)
    scale = jnp.exp(tops - top[None])
    return top, jnp.sum(sums * scale, axis=0), jnp.sum(extras * scale, axis=0), jnp.sum(extras, axis=0)


def kernel(
    n, rows,
    th_hbm, sh_hbm, wt_hbm, ws_hbm, ids_hbm, mask_hbm,
    tok_ref, loss_ref, hid_ref, head_ref,
    th_ref, sh_ref, ids_ref, mask_ref,
    own, gat, wt, ws, wtt, wst, xt, xs, part, diff, unit, hop_s, hop_d, hop_u, inc_s, inc_d, inc_u, sta, stb, tta, ttb, gb, grad, coef, lossb,
    ht, sibr, sb, rb, sc, rc,
    lsem, sent, r1, r2, r3, r4, r5, r6, rx, rg, rs,
):
    width = wt.shape[1]
    v = lax.axis_index("vocab")
    x = lax.axis_index("dp")
    c = lax.rem(v, 2)
    y = lax.rem(v // 2, n)
    z = v // (2 * n)
    sibling = 1 - c

    def dev(zz, yy, cc, xx=None):
        return ((zz * n + yy) * 2 + cc, x if xx is None else xx)

    def remote(src, dst, send, recv, device):
        return pltpu.make_async_remote_copy(
            src_ref=src, dst_ref=dst, send_sem=send, recv_sem=recv,
            device_id=device, device_id_type=pl.DeviceIdType.MESH,
        )

    def each(count, body, start=1):
        lax.fori_loop(start, count, lambda i, carry: (body(i), carry)[1], 0)

    def step(pos, d):
        return lax.rem(pos + d, n)

    first_s, second_s, swap_s, core_s, outer_s, inner_s, stat_a_s, stat_b_s, loss_s, g_s, logit_s, diff_s, teacher_a_s, teacher_b_s, coef_s, unit_s = (
        sent.at[i] for i in range(16)
    )

    def await_bytes(view, sem):
        pltpu.make_async_copy(view, view, sem).wait()

    pair = y * 2 + c

    def group_dev(d):
        other = lax.rem(pair + d, 2 * n)
        return dev(z, other // 2, lax.rem(other, 2))

    barrier = pltpu.get_barrier_semaphore()

    def greet(device):
        pl.semaphore_signal(barrier, inc=1, device_id=device, device_id_type=pl.DeviceIdType.MESH)

    each(n, lambda d: greet(dev(step(z, d), y, c)))
    each(2 * n, lambda d: greet(group_dev(d)))
    each(NX, lambda d: greet(dev(z, y, c, lax.rem(x + d, NX))))

    local = [
        pltpu.make_async_copy(src, dst, lsem.at[i])
        for i, (src, dst) in enumerate((
            (th_hbm, th_ref), (sh_hbm, sh_ref), (wt_hbm, wt), (ws_hbm, ws), (ids_hbm, ids_ref), (mask_hbm, mask_ref),
        ))
    ]
    for i in range(6):
        local[i].start()

    chunk = [lax.rem(x + d, NX) for d in (2, 1, 3, 0)]
    right, left = chunk[1], chunk[2]
    local[0].wait()
    local[1].wait()
    for rel in range(NX):
        lanes = pl.ds(pl.multiple_of(chunk[rel] * LANES, LANES), LANES)
        block = jnp.concatenate([th_ref[:, lanes].astype(F32), sh_ref[:, lanes].astype(F32)], axis=0)
        own[rel] = block.astype(BF16)
    flip = c
    p, q = (1 - flip) * z + flip * y, (1 - flip) * y + flip * z

    def along_p(d):
        return dev(step(z, d * (1 - flip)), step(y, d * flip), c)

    def along_q(d):
        return dev(step(z, d * flip), step(y, d * (1 - flip)), c)

    def first(cut, sem, d):
        return remote(own.at[cut], gat.at[cut, c, p, q], first_s, sem, along_q(d))

    def second(rel, sem, d):
        return remote(gat.at[rel, c, p], gat.at[rel, c, p], second_s, r2.at[rel, sem], along_p(d))

    def swap(rel, d):
        at = lax.rem(p + n - d, n)
        return remote(gat.at[rel, c, at], gat.at[rel, c, at], swap_s, r3.at[rel], dev(z, y, sibling))

    pl.semaphore_wait(barrier, (2 * n - 1) + (n - 1) + (NX - 1))

    ones = (
        lax.broadcasted_iota(jnp.int32, (LANES, LANES), 0) == lax.broadcasted_iota(jnp.int32, (LANES, LANES), 1)
    ).astype(BF16)

    def turn(load, src, dst):
        local[load].wait()

        def block(i):
            at = pl.ds(pl.multiple_of(i * LANES, LANES), LANES)
            dst[at, :] = lax.dot_general(
                ones, src[:, at], (((1,), (1,)), ((), ())), preferred_element_type=F32
            ).astype(BF16)

        each(width // LANES, block, 0)

    near = [d for d in range(1, n) if min(d, n - d) <= n // 4]
    far = [d for d in range(1, n) if d not in near]
    lead, rest = slice(0, 1), slice(1, NX)
    each(n, lambda d: first(lead, r1.at[0], d).start())
    each(n, lambda d: first(rest, r1.at[1], d).start())
    for rel in range(NX):
        gat[rel, c, p, q] = own[rel]

    def spread(rel):
        for d in far:
            second(rel, 1, d).start()
        for d in near:
            second(rel, 0, d).start()
        swap(rel, 0).start()

    turn(3, ws, wst)
    await_bytes(gat.at[lead, 0, 0, 0 : n - 1], r1.at[0])
    spread(0)
    await_bytes(gat.at[rest, 0, 0, 0 : n - 1], r1.at[1])
    for rel in range(1, NX):
        spread(rel)

    turn(2, wt, wtt)
    local[4].wait()
    local[5].wait()
    half = width // 2
    upper, lower = slice(0, half), slice(half, width)

    def logits(rel, after_student=lambda: None):
        for sem, group in ((0, near), (1, far)):
            if group:
                await_bytes(gat.at[rel, 0, 0 : len(group)], r2.at[rel, sem])
            for d in group:
                swap(rel, d).start()
        await_bytes(gat.at[rel, 0], r3.at[rel])

        columns = slice(rel * LANES, (rel + 1) * LANES)

        def place(half_tile, dst, i):
            halves = [gat[rel, 0, i].astype(F32)[:, half_tile], gat[rel, 1, :, i].astype(F32)[:, half_tile]]
            at = pl.ds(pl.multiple_of(i * (n * 16), n * 16), n * 16)
            dst[at] = jnp.stack(halves, axis=1).reshape(n * 16, LANES).astype(BF16)

        each(n, functools.partial(place, slice(8, 16), xs.at[:, columns]), 0)
        student = jnp.dot(wst[...], xs[:, columns], preferred_element_type=F32)
        part[rel, 1] = student
        after_student()
        each(n, functools.partial(place, slice(0, 8), xt), 0)
        part[rel, 0] = student - jnp.dot(wtt[...], xt[...], preferred_element_type=F32)
        if rel == 0:
            diff[0], unit[0] = code(part[0, 0])
        elif rel < NX - 1:
            early_rows = lower if rel == 1 else upper
            diff[rel, early_rows], unit[rel] = code(part[rel, 0, early_rows])

    def ring(src, dst, send, recv, to):
        return remote(src, dst, send, recv, dev(z, y, c, to))

    def hop_pair(cut, way, to):
        return [
            ring(part.at[0, 1, cut], hop_s.at[way], logit_s, rx.at[way], to),
            ring(unit.at[0], hop_u.at[way], unit_s, rx.at[6 + way], to),
            ring(diff.at[0, cut], hop_d.at[way], diff_s, rx.at[2 + way], to),
        ]

    def last_pair(rel, cut, way, to, unit_at):
        return [
            ring(part.at[rel, 1, cut], inc_s.at[way, cut], logit_s, rx.at[4], to),
            ring(unit.at[unit_at], inc_u.at[way, 0 if cut == upper else 1], unit_s, rx.at[8], to),
            ring(diff.at[rel, cut], inc_d.at[way, cut], diff_s, rx.at[5], to),
        ]

    hops = [hop_pair(upper, 0, right), hop_pair(lower, 1, left)]
    early = [last_pair(1, lower, 0, right, 1), last_pair(2, upper, 1, left, 2)]
    late = [last_pair(1, upper, 0, right, 3), last_pair(2, lower, 1, left, 4)]

    def start(*copies):
        for copy in copies:
            copy.start()

    def add_hop(way, rel, cut):
        hops[way][0].wait_recv()
        part[rel, 1, cut] = part[rel, 1, cut] + hop_s[way]
        late[way][0].start()
        hops[way][1].wait_recv()
        hops[way][2].wait_recv()
        diff[rel, cut], unit[3 + way] = code(part[rel, 0, cut] + decode(hop_d[way], hop_u[way]))
        start(*late[way][1:])

    logits(0, lambda: start(hops[0][0], hops[1][0]))
    start(*hops[0][1:], *hops[1][1:])
    logits(1, lambda: start(early[0][0]))
    start(*early[0][1:])
    logits(2, lambda: start(early[1][0]))
    start(*early[1][1:])
    add_hop(0, 1, upper)
    add_hop(1, 2, lower)
    logits(3)
    await_bytes(inc_s, rx.at[4])
    await_bytes(inc_d, rx.at[5])
    await_bytes(inc_u, rx.at[8])
    s = part[3, 1] + inc_s[0] + inc_s[1]
    gap = jnp.concatenate(
        [
            part[3, 0, cut] + decode(inc_d[0, cut], inc_u[0, k]) + decode(inc_d[1, cut], inc_u[1, k])
            for k, cut in enumerate((upper, lower))
        ],
        axis=0,
    )

    def stat_a(buf, send, sem, d):
        return remote(buf.at[pair], buf.at[pair], send, sem, group_dev(d))

    def stat_b(buf, send, sem, d):
        return remote(buf.at[z], buf.at[z], send, sem, dev(step(z, d), y, c))

    def send_a(buf, send, sem, parts):
        buf[pair] = jnp.concatenate(parts, axis=1)
        each(2 * n, lambda d: stat_a(buf, send, sem, d).start())

    def send_b(buf, send, sem, parts):
        buf[z] = jnp.concatenate(parts, axis=1)
        each(n, lambda d: stat_b(buf, send, sem, d).start())

    def slot(i):
        return slice(i * LANES, (i + 1) * LANES)

    quarter = half // 2
    cuts = [slice(k * quarter, (k + 1) * quarter) for k in range(4)]

    def g_copy(i, part_rows, source, target, to):
        return ring(gb.at[:, part_rows, slot(source)], gb.at[:, part_rows, slot(target)], g_s, rg.at[i], to)

    g_lead = [
        g_copy(0, cuts[0], 3, 2, right),
        g_copy(1, cuts[2], 3, 1, left),
        g_copy(2, cuts[1], 3, 2, right),
        g_copy(3, cuts[3], 3, 1, left),
    ]
    g_rest = [g_copy(4, lower, 3, 2, right), g_copy(5, upper, 3, 1, left)]
    g_relay = [
        g_copy(6, cuts[0], 2, 0, right),
        g_copy(6, cuts[2], 1, 0, left),
        g_copy(6, cuts[1], 2, 0, right),
        g_copy(6, cuts[3], 1, 0, left),
    ]
    m_s = jnp.max(s, axis=0, keepdims=True)
    e_s = jnp.exp(s - m_s)
    l_s = jnp.sum(e_s, axis=0, keepdims=True)
    k_s = jnp.sum(e_s * gap, axis=0, keepdims=True)
    send_a(sta, stat_a_s, rs.at[0], (m_s, l_s, k_s))
    own_top, own_mean = m_s, k_s / l_s
    gb[0, :, slot(3)] = e_s.astype(BF16)
    gb[1, :, slot(3)] = (e_s * (gap - own_mean)).astype(BF16)
    start(*g_lead, *g_rest)
    t = s - gap
    m_t = jnp.max(t, axis=0, keepdims=True)
    l_t = jnp.sum(jnp.exp(t - m_t), axis=0, keepdims=True)
    is_label = lax.broadcasted_iota(jnp.int32, (width, LANES), 0) == ids_ref[...] - v * width
    label = jnp.sum(jnp.where(is_label, s, 0.0), axis=0, keepdims=True)
    send_a(tta, teacher_a_s, rs.at[3], (m_t, l_t, label))
    await_bytes(sta.at[0 : 2 * n - 1], rs.at[0])
    send_b(stb, stat_b_s, rs.at[1], combine(sta[...])[:3])
    for k in range(4):
        g_lead[k].wait_recv()
        g_relay[k].start()
    await_bytes(tta.at[0 : 2 * n - 1], rs.at[3])
    m_t, l_t, _, label = combine(tta[...])
    send_b(ttb, teacher_b_s, rs.at[4], (m_t, l_t, label))
    await_bytes(stb.at[0 : n - 1], rs.at[1])
    m_s, l_s, k_s, _ = combine(stb[...])
    lse_s = m_s + jnp.log(l_s)
    mean_gap = k_s / l_s
    weights = mask_ref[...].astype(F32)
    factor = weights * jnp.exp(own_top - lse_s)
    coef[3] = jnp.concatenate([factor, factor * (mean_gap - own_mean), jnp.zeros((6, LANES), F32)], axis=0)
    coef_copies = [
        ring(coef.at[3], coef.at[0], coef_s, rs.at[5], chunk[0]),
        ring(coef.at[3], coef.at[2], coef_s, rs.at[7], right),
        ring(coef.at[3], coef.at[1], coef_s, rs.at[6], left),
    ]
    start(*coef_copies)

    def gradient(i):
        scale, shift = coef[i, 0:1], coef[i, 1:2]
        grad[:, slot(i)] = (
            scale * gb[1, :, slot(i)].astype(F32) - shift * gb[0, :, slot(i)].astype(F32)
        ).astype(BF16)

    def loss_copy(d):
        return remote(lossb.at[x], lossb.at[x], loss_s, rs.at[2], dev(z, y, c, lax.rem(x + d, NX)))

    def send_loss():
        await_bytes(ttb.at[0 : n - 1], rs.at[4])
        m_t, l_t, _, label = combine(ttb[...])
        tok_ref[...] = label - lse_s
        row_kl = mean_gap - lse_s + m_t + jnp.log(l_t)
        lossb[x] = jnp.broadcast_to(weights * row_kl, (8, LANES))
        each(NX, lambda d: loss_copy(d).start())

    def core_copy(i):
        return remote(ht.at[i, :, sibling], sibr.at[i], core_s, r4.at[i], dev(z, y, sibling))

    def terms(i):
        gradient(i)
        ht[i] = jnp.dot(ws[...], grad[:, slot(i)], preferred_element_type=F32).reshape(n * n, 2, 8, LANES)
        core_copy(i).start()

    def outer(i, d):
        return remote(sb.at[i, step(p, d)], rb.at[i, p], outer_s, r5.at[i], along_p(d))

    def inner(i, d):
        return remote(sc.at[i, step(q, d)], rc.at[i, q], inner_s, r6.at[i], along_q(d))

    def send_outer(i):
        core_copy(i).wait_recv()
        total = (ht[i, :, c] + sibr[i]).reshape(n, n, 8, LANES)
        for k in range(n):
            piece = jnp.where(c == 0, total[k], total[:, k])
            sb[i, k] = piece.reshape(n * 8, LANES).astype(BF16)
        each(n, lambda d: outer(i, d).start())
        rb[i, p] = sb[i, p]

    def send_inner(i):
        await_bytes(rb.at[i, 0 : n - 1], r5.at[i])
        sc[i] = jnp.sum(rb[i].astype(F32), axis=0).reshape(n, 8, LANES)
        each(n, lambda d: inner(i, d).start())
        rc[i, q] = sc[i, q]

    def finish(i):
        await_bytes(rc.at[i, 0 : n - 1], r6.at[i])
        lanes = pl.ds(pl.multiple_of(chunk[i] * LANES, LANES), LANES)
        hid_ref[:, lanes] = jnp.sum(rc[i], axis=0)

    terms(3)
    send_loss()
    send_outer(3)
    g_rest[0].wait_recv()
    coef_copies[1].wait_recv()
    terms(2)
    g_rest[1].wait_recv()
    coef_copies[2].wait_recv()
    terms(1)
    await_bytes(gb.at[:, :, slot(0)], rg.at[6])
    coef_copies[0].wait_recv()
    terms(0)
    for i in (2, 1, 0):
        send_outer(i)
    await_bytes(lossb.at[0 : NX - 1], rs.at[2])
    loss = jnp.sum(lossb[:, 0:1].reshape(NX, LANES)) / rows
    loss_ref[...] = jnp.full((1, LANES), loss, F32)
    head_ref[...] = lax.dot_general(
        xs[...], grad[...], (((1,), (1,)), ((), ())), preferred_element_type=F32
    ).astype(BF16)
    for i in (3, 2, 1, 0):
        send_inner(i)
    for i in (3, 2, 1, 0):
        finish(i)

    for view, sem in (
        (gat.at[:, 0, 0, 0 : n - 1], first_s),
        (gat.at[:, 0, 0 : n - 1], second_s),
        (gat.at[:, 0], swap_s),
        (sibr, core_s),
        (sb.at[:, 0 : n - 1], outer_s),
        (sc.at[:, 0 : n - 1], inner_s),
        (sta.at[0 : 2 * n - 1], stat_a_s),
        (tta.at[0 : 2 * n - 1], teacher_a_s),
        (stb.at[0 : n - 1], stat_b_s),
        (ttb.at[0 : n - 1], teacher_b_s),
        (lossb.at[0 : NX - 1], loss_s),
        (gb.at[:, :, 0 : 3 * LANES], g_s),
        (coef.at[0 : NX - 1], coef_s),
        (part.at[0 : NX - 1, 1], logit_s),
        (diff, diff_s),
        (unit, unit_s),
    ):
        await_bytes(view, sem)


def store(tok_ref, loss_ref, hid_ref, head_ref, tok_out, loss_out, hid_out, head_out, one, rounded, sems):
    copies = [
        pltpu.make_async_copy(src, dst, sems.at[i])
        for i, (src, dst) in enumerate(
            ((head_ref, head_out), (tok_ref, tok_out), (one, loss_out), (rounded, hid_out))
        )
    ]
    copies[0].start()
    copies[1].start()
    one[...] = loss_ref[:, 0:1]
    rounded[...] = hid_ref[...].astype(BF16)
    copies[2].start()
    copies[3].start()
    for copy in copies:
        copy.wait()


def shards(n, teacher_hidden, student_hidden, teacher_head, student_head, token_ids, row_mask):
    rows = teacher_hidden.shape[0]
    depth, width = teacher_head.shape
    hbm = pl.BlockSpec(memory_space=pl.ANY)
    dma = pltpu.SemaphoreType.DMA
    scratch = [
        pltpu.VMEM((8, rows), BF16),
        pltpu.VMEM((8, rows), BF16),
        pltpu.VMEM((1, LANES), jnp.int32),
        pltpu.VMEM((1, LANES), jnp.int32),
        pltpu.VMEM((NX, 16, LANES), BF16),
        pltpu.VMEM((NX, 2, n, n, 16, LANES), BF16),
        pltpu.VMEM((depth, width), BF16),
        pltpu.VMEM((depth, width), BF16),
        pltpu.VMEM((width, depth), BF16),
        pltpu.VMEM((width, depth), BF16),
        pltpu.VMEM((depth, LANES), BF16),
        pltpu.VMEM((depth, rows), BF16),
        pltpu.VMEM((NX, 2, width, LANES), F32),
        pltpu.VMEM((NX - 1, width, LANES), jnp.int16),
        pltpu.VMEM((6, 8, LANES), F32),
        pltpu.VMEM((2, width // 2, LANES), F32),
        pltpu.VMEM((2, width // 2, LANES), jnp.int16),
        pltpu.VMEM((2, 8, LANES), F32),
        pltpu.VMEM((2, width, LANES), F32),
        pltpu.VMEM((2, width, LANES), jnp.int16),
        pltpu.VMEM((2, 2, 8, LANES), F32),
        pltpu.VMEM((2 * n, 1, 3 * LANES), F32),
        pltpu.VMEM((n, 1, 3 * LANES), F32),
        pltpu.VMEM((2 * n, 1, 3 * LANES), F32),
        pltpu.VMEM((n, 1, 3 * LANES), F32),
        pltpu.VMEM((2, width, rows), BF16),
        pltpu.VMEM((width, rows), BF16),
        pltpu.VMEM((NX, 8, LANES), F32),
        pltpu.VMEM((NX, 8, LANES), F32),
        pltpu.VMEM((NX, n * n, 2, 8, LANES), F32),
        pltpu.VMEM((NX, n * n, 8, LANES), F32),
        pltpu.VMEM((NX, n, n * 8, LANES), BF16),
        pltpu.VMEM((NX, n, n * 8, LANES), BF16),
        pltpu.VMEM((NX, n, 8, LANES), F32),
        pltpu.VMEM((NX, n, 8, LANES), F32),
        dma((6,)), dma((16,)), dma((2,)), dma((NX, 2)), dma((NX,)), dma((NX,)), dma((NX,)), dma((NX,)),
        dma((9,)), dma((7,)), dma((8,)),
    ]
    tok, loss, hidden, head = pl.pallas_call(
        functools.partial(kernel, n, rows),
        out_shape=(
            pltpu.VMEM((1, LANES), F32),
            pltpu.VMEM((1, LANES), F32),
            pltpu.VMEM((8, rows), F32),
            pltpu.VMEM((depth, width), BF16),
        ),
        in_specs=[hbm] * 6,
        out_specs=(pl.BlockSpec(memory_space=pltpu.VMEM),) * 4,
        scratch_shapes=scratch,
        compiler_params=pltpu.CompilerParams(
            collective_id=0, has_side_effects=True, vmem_limit_bytes=60 * 1024 * 1024
        ),
        cost_estimate=pl.CostEstimate(flops=6 * 10**9, bytes_accessed=5 * 10**6, transcendentals=3 * 10**5),
    )(
        teacher_hidden.T, student_hidden.T, teacher_head, student_head,
        token_ids.reshape(1, LANES), row_mask.reshape(1, LANES),
    )
    vmem = pl.BlockSpec(memory_space=pltpu.VMEM)
    tok, loss, hidden, head = pl.pallas_call(
        store,
        out_shape=(
            jax.ShapeDtypeStruct((1, LANES), F32),
            jax.ShapeDtypeStruct((1, 1), F32),
            jax.ShapeDtypeStruct((8, rows), BF16),
            jax.ShapeDtypeStruct((depth, width), BF16),
        ),
        in_specs=[vmem] * 4,
        out_specs=(hbm,) * 4,
        scratch_shapes=[pltpu.VMEM((1, 1), F32), pltpu.VMEM((8, rows), BF16), dma((4,))],
        compiler_params=pltpu.CompilerParams(vmem_limit_bytes=4 * 1024 * 1024),
    )(tok, loss, hidden, head)
    return (tok.reshape(LANES), loss.reshape(()), hidden.T, head)


def solution(mesh):
    side = int(round((mesh.shape["vocab"] // 2) ** 0.5))
    placed = (
        P(None, ("dp", "vocab")),
        P(None, ("dp", "vocab")),
        P("dp", "vocab"),
        P("dp", "vocab"),
        P("dp"),
        P("dp"),
    )
    return jax.shard_map(
        functools.partial(shards, side),
        mesh=mesh,
        in_specs=placed,
        out_specs=(P("dp"), P(), P(None, ("dp", "vocab")), P("dp", "vocab")),
        check_vma=False,
    )
```
